256 devices in a mesh: view: 4 (over z_lo), clip: 64 (over z_hi, y, x, core).
Axes of the slice: x: 4, y: 4, z: 8 (z_hi: 2, z_lo: 4; z = z_hi * 4 + z_lo), core: 2. Of those that a mesh axis runs over, the one named last changes fastest.
Arguments:
- queries: bfloat16 [4, 16384, 1536], P('view', 'clip'), may hold values from -20 to 20
- keys: bfloat16 [4, 16384, 1536], P('view', 'clip'), may hold values from -20 to 20
- values: bfloat16 [4, 16384, 1536], P('view', 'clip'), may hold values from -6 to 6
- out_grad: bfloat16 [4, 16384, 1536], P('view', 'clip'), may hold values from -6 to 6
- counts: int32 [4, 64], P('view', 'clip'), may hold values from 64 to 256, as said below
- camera_pairs: int32 [4, 2], replicated, may hold values from 0 to 3, as said below
Outputs:
- attended: bfloat16 [4, 16384, 1536], P('view', 'clip')
- query_grad: bfloat16 [4, 16384, 1536], P('view', 'clip')
- key_grad: bfloat16 [4, 16384, 1536], P('view', 'clip')
- value_grad: bfloat16 [4, 16384, 1536], P('view', 'clip')
The draws below stay inside these ranges and needn't reach their ends.
Inputs may be any that keep to these rules, and one draw needn't show every extreme that they name: `camera_pairs`: row j names two cameras; the rows form one cycle through all 4 cameras, so every camera stands once in the first column and once in the second, with two different partners. `counts`: some camera's clip segment holds all 256 tokens.
All inputs are finite; a program needn't handle non-finite values.
Results may differ from the reference program's by a relative error of at most 0.012.
The reference program's roundings to bfloat16 on the way (of `weights_low` and `dscores`) count: a program that leaves them out, or rounds other values in their place, can miss the bound.
Values may be sent and summed in bfloat16 or wider, within the bound.
No kernel may reach another device: no remote copies, remote signals or barrier semaphores. Data moves between devices by JAX's collectives and lax.ppermute only.
A program may use at most 128 MiB of HBM per device.

```python
import math
import jax
import jax.numpy as jnp
from jax import lax

D = 1536
H = 12
HD = 128
CT = 256
W = 2
NV = 4
NCHUNK = 64


def shared_field(key):
    base = jax.random.normal(key, (NV, NCHUNK * CT, D), jnp.float32)
    return jnp.clip(base, -4.0, 4.0)


def draw_keys(key, part):
    base = shared_field(key)
    return base.astype(jnp.bfloat16)


def draw_queries(key, part):
    key = jax.random.fold_in(key, 5)
    return jnp.clip(jax.random.normal(key, (NV, NCHUNK * CT, D), jnp.float32), -4.0, 4.0).astype(jnp.bfloat16)


def draw_counts(key, part):
    key = jax.random.fold_in(key, 7)
    first_key, second_key = jax.random.split(key)
    drawn = jax.random.randint(first_key, (NV * NCHUNK,), CT // 4, CT + 1, jnp.int32)
    full_place = jax.random.randint(second_key, (), 0, NV * NCHUNK, jnp.int32)
    drawn = jnp.where(jnp.arange(NV * NCHUNK) == full_place, CT, drawn)
    return drawn.reshape(NV, NCHUNK).astype(jnp.int32)


def draw_camera_pairs(key, part):
    key = jax.random.fold_in(key, 9)
    order = jax.random.permutation(key, NV).astype(jnp.int32)
    return jnp.stack([order, jnp.roll(order, -1)], axis=1).astype(jnp.int32)


def level_of(key, shape, cuts, smallest, high):
    loudness, own = 1.0, jax.random.fold_in(key, 6)
    for axis_at, parts in cuts:
        steps = jnp.exp(jax.random.uniform(jax.random.fold_in(own, axis_at), (parts,), jnp.float32, smallest / len(cuts), high / len(cuts)))
        loudness = loudness * jnp.repeat(steps, shape[axis_at] // parts).reshape([-1 if axis == axis_at else 1 for axis in range(len(shape))])
    return loudness


def gaussian(stream_key, extent, scale, limit, shards=(), kind=jnp.bfloat16):
    entries = jax.random.normal(stream_key, extent, jnp.float32) * scale
    if len(shards) > 0:
        entries = level_of(stream_key, extent, shards, -0.22, 0.18) * entries
    return jnp.clip(entries, min=-limit, max=limit).astype(kind)


def setup_inputs(seed: int = 0) -> dict:
    key_of = jax.random.split(jax.random.key(seed), 7)
    queries = draw_queries(jax.random.fold_in(key_of[6], 71), 0)
    keys = draw_keys(jax.random.fold_in(key_of[6], 71), 0)
    values = gaussian(key_of[2], (NV, NCHUNK * CT, D), 1.0, 6.0, ((0, 4), (1, 64)))
    out_grad = gaussian(key_of[3], (NV, NCHUNK * CT, D), 1.0, 6.0, ((0, 4), (1, 64)))
    counts = draw_counts(jax.random.fold_in(key_of[6], 71), 0)
    camera_pairs = draw_camera_pairs(jax.random.fold_in(key_of[6], 71), 0)
    return {"queries": queries, "keys": keys, "values": values, "out_grad": out_grad, "counts": counts, "camera_pairs": camera_pairs}


MASKED = -1e+30

def attend_block(query_rows, grad_rows, key_rows, value_rows, key_valid):
    factor = 1.0 / math.sqrt(HD)
    count_rows = query_rows.shape[0]
    count_keys = key_rows.shape[0]
    head_q = query_rows.astype(jnp.float32).reshape(count_rows, H, HD)
    head_g = grad_rows.astype(jnp.float32).reshape(count_rows, H, HD)
    head_k = key_rows.astype(jnp.float32).reshape(count_keys, H, HD)
    head_v = value_rows.astype(jnp.float32).reshape(count_keys, H, HD)
    scores = jnp.einsum('qhd,khd->hqk', head_q, head_k) * factor
    scores = jnp.where(key_valid[None, None, :], scores, MASKED)
    row_max = lax.optimization_barrier(jnp.max(scores, axis=2, keepdims=True))
    log_total = row_max + jnp.log(lax.optimization_barrier(jnp.sum(jnp.exp(scores - row_max), axis=2, keepdims=True)))
    weights = jnp.exp(scores - log_total)
    weights_low = weights.astype(jnp.bfloat16).astype(jnp.float32)
    attended = jnp.einsum('hqk,khd->qhd', weights_low, head_v).astype(jnp.bfloat16)
    row_delta = lax.optimization_barrier(jnp.sum(head_g * attended.astype(jnp.float32), axis=2)).T
    dweights = jnp.einsum('qhd,khd->hqk', head_g, head_v)
    dscores = (weights * (dweights - row_delta[:, :, None])).astype(jnp.bfloat16).astype(jnp.float32)
    query_grad = (jnp.einsum('hqk,khd->qhd', dscores, head_k) * factor).astype(jnp.bfloat16)
    key_term = (jnp.einsum('hqk,qhd->khd', dscores, head_q) * factor).astype(jnp.bfloat16)
    value_term = jnp.einsum('hqk,qhd->khd', weights_low, head_g).astype(jnp.bfloat16)
    terms = jnp.concatenate([key_term.reshape(count_keys, D), value_term.reshape(count_keys, D)], axis=1)
    return (attended.reshape(count_rows, D), query_grad.reshape(count_rows, D), terms.astype(jnp.float32))

def reference(queries, keys, values, out_grad, counts, camera_pairs):
    zero_index = jnp.zeros((), jnp.int32)

    def block_of(array, camera, segment):
        start = (segment * CT).astype(jnp.int32)
        return lax.dynamic_slice(array, (camera.astype(jnp.int32), start, zero_index), (1, CT, D))[0]

    def step(totals, block_index):
        camera = (block_index // NCHUNK).astype(jnp.int32)
        segment = (block_index % NCHUNK).astype(jnp.int32)
        left_view = jnp.sum(jnp.where(camera_pairs[:, 0] == camera, camera_pairs[:, 1], 0)).astype(jnp.int32)
        right_view = jnp.sum(jnp.where(camera_pairs[:, 1] == camera, camera_pairs[:, 0], 0)).astype(jnp.int32)
        source_views = [camera] * (W + 1) + [left_view, right_view]
        source_segments = [segment - distance for distance in range(W + 1)] + [segment, segment]
        key_list, value_list, valid_list, places = ([], [], [], [])
        for source_view, source_segment in zip(source_views, source_segments):
            alive = source_segment >= 0
            clamped = jnp.maximum(source_segment, 0).astype(jnp.int32)
            live_count = jnp.where(alive, counts[source_view, clamped], 0)
            key_list.append(block_of(keys, source_view, clamped))
            value_list.append(block_of(values, source_view, clamped))
            valid_list.append(jnp.arange(CT) < live_count)
            places.append((source_view, clamped))
        attended, query_grad, terms = attend_block(block_of(queries, camera, segment), block_of(out_grad, camera, segment), jnp.concatenate(key_list, axis=0), jnp.concatenate(value_list, axis=0), jnp.concatenate(valid_list, axis=0))
        for position, (source_view, clamped) in enumerate(places):
            totals = totals.at[source_view, clamped].add(terms[position * CT:(position + 1) * CT])
        return (totals, (attended, query_grad))
    start_totals = jnp.zeros((NV, NCHUNK, CT, 2 * D), jnp.float32)
    totals, (attended, query_grad) = lax.scan(step, start_totals, jnp.arange(NV * NCHUNK, dtype=jnp.int32))
    grads = totals.astype(jnp.bfloat16).reshape(NV, NCHUNK * CT, 2 * D)
    return (attended.reshape(NV, NCHUNK * CT, D), query_grad.reshape(NV, NCHUNK * CT, D), grads[:, :, :D], grads[:, :, D:])
```

```python
import math

import jax
import jax.numpy as jnp
from jax import lax
from jax.experimental import pallas as pl
from jax.experimental.pallas import tpu as pltpu
from jax.sharding import PartitionSpec as P

H = 12
HD = 128
W = 2
NV = 4
CHUNKS = 3
PAD = 16

MASKED = -1e30
FACTOR = 1.0 / math.sqrt(HD)
LOG2E = math.log2(math.e)


def dot(a, b, side_a, side_b):
    return lax.dot_general(
        a, b, (((side_a,), (side_b,)), ((), ())), preferred_element_type=jnp.float32
    )


def head_kernel(q_ref, g_ref, *refs):
    packs, (o_ref, dq_ref, *term_refs) = refs[: W + 3], refs[-(W + 5) :]
    rows = q_ref.shape[0]
    q = q_ref[...]
    g = g_ref[...]
    place = lax.broadcasted_iota(jnp.int32, (rows, rows), 0).astype(jnp.float32)
    scores, top = [], None
    for pack in packs:
        s = dot(pack[0:rows, :], q, 1, 1) * (FACTOR * LOG2E)
        count = pack[2 * rows : 2 * rows + 1, :].astype(jnp.float32)
        count = jnp.concatenate([count] * (rows // HD), axis=1)
        s = jnp.where(place < count, s, MASKED)
        scores.append(s)
        high = jnp.max(s, axis=0, keepdims=True)
        top = high if top is None else jnp.maximum(top, high)
    total, powers = 0.0, []
    for s in scores:
        power = jnp.exp2(s - top)
        powers.append(power)
        total = total + jnp.sum(power, axis=0, keepdims=True)
    inverse = 1.0 / total
    weights = [power * inverse for power in powers]
    low = [w.astype(jnp.bfloat16) for w in weights]
    out = 0.0
    for pack, w in zip(packs, low):
        out = out + dot(pack[rows : 2 * rows, :], w, 0, 0)
    out = out.astype(jnp.bfloat16)
    delta = jnp.sum(g.T.astype(jnp.float32) * out.astype(jnp.float32), axis=0, keepdims=True)
    o_ref[...] = out.T
    dq = 0.0
    for pack, w, w_low, term in zip(packs, weights, low, term_refs):
        dw = dot(pack[rows : 2 * rows, :], g, 1, 1)
        ds = (w * (dw - delta)).astype(jnp.bfloat16)
        dq = dq + dot(pack[0:rows, :], ds, 0, 0)
        term[0:rows, :] = (dot(ds, q, 1, 0) * FACTOR).astype(jnp.bfloat16)
        term[rows : 2 * rows, :] = dot(w_low, g, 1, 0).astype(jnp.bfloat16)
    dq_ref[...] = (dq * FACTOR).astype(jnp.bfloat16).T


def attend(q, g, packs, earlier, chunk):
    rows, width = q.shape
    heads = H // CHUNKS
    in_whole = pl.BlockSpec((rows, HD), lambda h: (0, chunk * heads + h))
    in_pack = pl.BlockSpec((2 * rows + PAD, HD), lambda h: (0, h))
    term = pl.BlockSpec((2 * rows, HD), lambda h: (0, h))
    count = len(packs)
    arguments = [q, g, *packs]
    in_specs = [in_whole] * 2 + [in_pack] * count
    aliases = {}
    if earlier is not None:
        aliases = {count + 2: 0, count + 3: 1}
        arguments += list(earlier)
        in_specs += [pl.BlockSpec(memory_space=pl.ANY)] * 2
    results = pl.pallas_call(
        head_kernel,
        grid=(heads,),
        in_specs=in_specs,
        out_specs=[in_whole] * 2 + [term] * count,
        out_shape=[jax.ShapeDtypeStruct((rows, width), jnp.bfloat16)] * 2
        + [jax.ShapeDtypeStruct((2 * rows, heads * HD), jnp.bfloat16)] * count,
        input_output_aliases=aliases,
        cost_estimate=pl.CostEstimate(
            flops=heads * 20 * rows * rows * count * HD,
            bytes_accessed=heads * 8 * (count + 1) * rows * HD,
            transcendentals=heads * count * rows * rows,
        ),
        compiler_params=pltpu.CompilerParams(vmem_limit_bytes=40 * 1024 * 1024),
    )(*arguments)
    return results[:2], results[2:]


def add_kernel(count, *refs):
    terms, (dk_ref, dv_ref) = refs[:count], refs[-2:]
    rows = dk_ref.shape[0]
    for out, start in ((dk_ref, 0), (dv_ref, rows)):
        total = terms[0][start : start + rows, :].astype(jnp.float32)
        for term in terms[1:]:
            total = total + term[start : start + rows, :].astype(jnp.float32)
        out[...] = total.astype(jnp.bfloat16)


def add_up(terms, earlier, chunk, width):
    rows, part = terms[0].shape[0] // 2, terms[0].shape[1]
    count = len(terms)
    steps = part // HD
    in_specs = [pl.BlockSpec((2 * rows, HD), lambda h: (0, h))] * count
    arguments = list(terms)
    aliases = {}
    if earlier is not None:
        aliases = {count: 0, count + 1: 1}
        arguments += list(earlier)
        in_specs += [pl.BlockSpec(memory_space=pl.ANY)] * 2
    return pl.pallas_call(
        lambda *refs: add_kernel(count, *refs),
        grid=(steps,),
        in_specs=in_specs,
        out_specs=[pl.BlockSpec((rows, HD), lambda h: (0, chunk * steps + h))] * 2,
        out_shape=[jax.ShapeDtypeStruct((rows, width), jnp.bfloat16)] * 2,
        input_output_aliases=aliases,
        cost_estimate=pl.CostEstimate(
            flops=count * 2 * rows * part,
            bytes_accessed=4 * (count + 1) * rows * part,
            transcendentals=0,
        ),
        compiler_params=pltpu.CompilerParams(vmem_limit_bytes=40 * 1024 * 1024),
    )(*arguments)


def over_views(block, flip):
    return lax.ppermute(block, "view", [(i, i ^ flip) for i in range(NV)])


def over_clips(block, distance):
    clips = range(lax.axis_size("clip"))
    route = [(i, i + distance) for i in clips if i + distance in clips]
    return lax.ppermute(block, "clip", route)


def run(near, far, queries, keys, values, out_grad, counts):
    q, k, v, g = queries[0], keys[0], values[0], out_grad[0]
    rows, width = q.shape
    part = width // CHUNKS
    count_rows = jnp.full((PAD, part), counts[0, 0], jnp.bfloat16)
    packs = []
    for chunk in range(CHUNKS):
        columns = slice(chunk * part, (chunk + 1) * part)
        own = jnp.concatenate([k[:, columns], v[:, columns], count_rows], axis=0)
        across = over_views(own, far)
        beside = over_views(own if near else across, 1)
        packs.append([own] + [over_clips(own, d) for d in range(1, W + 1)] + [across, beside])
    outs = grads = None
    for chunk in range(CHUNKS):
        outs, terms = attend(q, g, packs[chunk], outs, chunk)
        own, across, beside = terms[0], terms[W + 1], terms[W + 2]
        gathered = [own] + [over_clips(terms[d], -d) for d in range(1, W + 1)]
        back = over_views(beside, 1)
        if near:
            gathered += [back, over_views(across, far)]
        else:
            both = (across.astype(jnp.float32) + back.astype(jnp.float32)).astype(jnp.bfloat16)
            gathered.append(over_views(both, far))
        grads = add_up(gathered, grads, chunk, width)
    return tuple(x[None] for x in (*outs, *grads))


def per_device(queries, keys, values, out_grad, counts, camera_pairs):
    first, second = camera_pairs[:, 0], camera_pairs[:, 1]
    met = jnp.sum(jnp.where(first == 0, second, 0)) + jnp.sum(jnp.where(second == 0, first, 0))
    apart = 6 - met
    plans = [(0, 2), (1, 3), (1, 2)]
    return lax.switch(
        apart - 1,
        [lambda *arrays, plan=plan: run(*plan, *arrays) for plan in plans],
        queries,
        keys,
        values,
        out_grad,
        counts,
    )


def solution(mesh):
    split = P("view", "clip", None)
    return jax.shard_map(
        per_device,
        mesh=mesh,
        in_specs=(split, split, split, split, P("view", "clip"), P()),
        out_specs=(split, split, split, split),
        check_vma=False,
    )
```

```python
import math

import jax
import jax.numpy as jnp
from jax import lax
from jax.experimental import pallas as pl
from jax.experimental.pallas import tpu as pltpu
from jax.sharding import PartitionSpec as P

H = 12
HD = 128
W = 2
NV = 4
CHUNKS = 3
PAD = 16

MASKED = -1e30
FACTOR = 1.0 / math.sqrt(HD)
LOG2E = math.log2(math.e)


def dot(a, b, side_a, side_b):
    return lax.dot_general(
        a, b, (((side_a,), (side_b,)), ((), ())), preferred_element_type=jnp.float32
    )


def head_kernel(q_ref, g_ref, *refs):
    packs, (o_ref, dq_ref, *term_refs) = refs[: W + 3], refs[-(W + 5) :]
    rows = q_ref.shape[0]
    q = q_ref[...]
    g = g_ref[...]
    place = lax.broadcasted_iota(jnp.int32, (rows, rows), 0).astype(jnp.float32)
    scores, top = [], None
    for pack in packs:
        s = dot(pack[0:rows, :], q, 1, 1) * (FACTOR * LOG2E)
        count = pack[2 * rows : 2 * rows + 1, :].astype(jnp.float32)
        count = jnp.concatenate([count] * (rows // HD), axis=1)
        s = jnp.where(place < count, s, MASKED)
        scores.append(s)
        high = jnp.max(s, axis=0, keepdims=True)
        top = high if top is None else jnp.maximum(top, high)
    total, powers = 0.0, []
    for s in scores:
        power = jnp.exp2(s - top)
        powers.append(power)
        total = total + jnp.sum(power, axis=0, keepdims=True)
    inverse = 1.0 / total
    weights = [power * inverse for power in powers]
    low = [w.astype(jnp.bfloat16) for w in weights]
    out = 0.0
    for pack, w in zip(packs, low):
        out = out + dot(pack[rows : 2 * rows, :], w, 0, 0)
    out = out.astype(jnp.bfloat16)
    delta = jnp.sum(g.T.astype(jnp.float32) * out.astype(jnp.float32), axis=0, keepdims=True)
    o_ref[...] = out.T
    dq = 0.0
    for pack, w, w_low, term in zip(packs, weights, low, term_refs):
        dw = dot(pack[rows : 2 * rows, :], g, 1, 1)
        ds = (w * (dw - delta)).astype(jnp.bfloat16)
        dq = dq + dot(pack[0:rows, :], ds, 0, 0)
        term[0:rows, :] = (dot(ds, q, 1, 0) * FACTOR).astype(jnp.bfloat16)
        term[rows : 2 * rows, :] = dot(w_low, g, 1, 0).astype(jnp.bfloat16)
    dq_ref[...] = (dq * FACTOR).astype(jnp.bfloat16).T


def attend(q, g, packs, earlier, chunk):
    rows, width = q.shape
    heads = H // CHUNKS
    in_whole = pl.BlockSpec((rows, HD), lambda h: (0, chunk * heads + h))
    in_pack = pl.BlockSpec((2 * rows + PAD, HD), lambda h: (0, h))
    term = pl.BlockSpec((2 * rows, HD), lambda h: (0, h))
    count = len(packs)
    arguments = [q, g, *packs]
    in_specs = [in_whole] * 2 + [in_pack] * count
    aliases = {}
    if earlier is not None:
        aliases = {count + 2: 0, count + 3: 1}
        arguments += list(earlier)
        in_specs += [pl.BlockSpec(memory_space=pl.ANY)] * 2
    results = pl.pallas_call(
        head_kernel,
        grid=(heads,),
        in_specs=in_specs,
        out_specs=[in_whole] * 2 + [term] * count,
        out_shape=[jax.ShapeDtypeStruct((rows, width), jnp.bfloat16)] * 2
        + [jax.ShapeDtypeStruct((2 * rows, heads * HD), jnp.bfloat16)] * count,
        input_output_aliases=aliases,
        cost_estimate=pl.CostEstimate(
            flops=heads * 20 * rows * rows * count * HD,
            bytes_accessed=heads * 8 * (count + 1) * rows * HD,
            transcendentals=heads * count * rows * rows,
        ),
        compiler_params=pltpu.CompilerParams(vmem_limit_bytes=40 * 1024 * 1024),
    )(*arguments)
    return results[:2], results[2:]


def add_kernel(count, even_ref, *refs):
    terms, (dk_ref, dv_ref) = refs[:count], refs[-2:]
    rows = dk_ref.shape[0]
    even = even_ref[0] == 1
    for out, start in ((dk_ref, 0), (dv_ref, rows)):
        handed = terms[0][start : start + rows, :].astype(jnp.float32)
        total = jnp.where(even, handed, 0.0)
        for term in terms[1:]:
            total = total + term[start : start + rows, :].astype(jnp.float32)
        out[...] = total.astype(jnp.bfloat16)


def add_up(terms, earlier, chunk, width):
    rows, part = terms[0].shape[0] // 2, terms[0].shape[1]
    count = len(terms)
    steps = part // HD
    even = (1 - lax.axis_index("clip") % 2).astype(jnp.int32).reshape(1)
    in_specs = [pl.BlockSpec(memory_space=pltpu.SMEM)]
    in_specs += [pl.BlockSpec((2 * rows, HD), lambda h: (0, h))] * count
    arguments = [even, *terms]
    aliases = {}
    if earlier is not None:
        aliases = {count + 1: 0, count + 2: 1}
        arguments += list(earlier)
        in_specs += [pl.BlockSpec(memory_space=pl.ANY)] * 2
    return pl.pallas_call(
        lambda *refs: add_kernel(count, *refs),
        grid=(steps,),
        in_specs=in_specs,
        out_specs=[pl.BlockSpec((rows, HD), lambda h: (0, chunk * steps + h))] * 2,
        out_shape=[jax.ShapeDtypeStruct((rows, width), jnp.bfloat16)] * 2,
        input_output_aliases=aliases,
        cost_estimate=pl.CostEstimate(
            flops=count * 2 * rows * part,
            bytes_accessed=4 * (count + 1) * rows * part,
            transcendentals=0,
        ),
        compiler_params=pltpu.CompilerParams(vmem_limit_bytes=40 * 1024 * 1024),
    )(*arguments)


def over_views(block, flip):
    return lax.ppermute(block, "view", [(i, i ^ flip) for i in range(NV)])


def over_clips(block, route):
    return lax.ppermute(block, "clip", route)


def clip_at(z_hi, y, x, core):
    return ((z_hi * 4 + y) * 4 + x) * 2 + core


EDGE = 32
FORWARD_RELAYS = [
    (clip_at(0, 3, 3, 0), clip_at(0, 2, 3, 1)),
    (clip_at(0, 3, 2, 0), clip_at(0, 3, 0, 1)),
    (clip_at(0, 0, 3, 0), clip_at(0, 0, 0, 1)),
]
RETURN_RELAYS = [
    (clip_at(1, 2, 0, 0), clip_at(1, 0, 2, 1)),
    (clip_at(1, 0, 1, 0), clip_at(1, 1, 1, 1)),
    (clip_at(1, 0, 0, 0), clip_at(1, 1, 0, 1)),
]


def two_on(block, relays):
    clips = range(lax.axis_size("clip") - 2)
    within = over_clips(block, [(i, i + 2) for i in clips if i + 2 not in (EDGE, EDGE + 1)])
    relayed = over_clips(block, list(zip((EDGE - 2, EDGE - 1), relays)))
    return within, over_clips(relayed, list(zip(relays, (EDGE, EDGE + 1))))


def two_back(block, relays):
    clips = range(lax.axis_size("clip") - 2)
    within = over_clips(block, [(i + 2, i) for i in clips if i + 2 not in (EDGE, EDGE + 1)])
    relayed = over_clips(block, list(zip((EDGE, EDGE + 1), relays)))
    return within, over_clips(relayed, list(zip(relays, (EDGE - 2, EDGE - 1))))


def swap_cores(block):
    return over_clips(block, [(i, i ^ 1) for i in range(lax.axis_size("clip"))])


def run(near, far, queries, keys, values, out_grad, counts):
    q, k, v, g = queries[0], keys[0], values[0], out_grad[0]
    rows, width = q.shape
    part = width // CHUNKS
    clip = lax.axis_index("clip")
    odd = clip % 2 == 1
    after_edge = (clip == EDGE) | (clip == EDGE + 1)
    count_rows = jnp.full((PAD, part), counts[0, 0], jnp.bfloat16)
    packs = []
    for chunk in range(CHUNKS):
        columns = slice(chunk * part, (chunk + 1) * part)
        own = jnp.concatenate([k[:, columns], v[:, columns], count_rows], axis=0)
        across = over_views(own, far)
        within, crossed = two_on(own, FORWARD_RELAYS[chunk])
        second = jnp.where(after_edge, crossed, within)
        first = swap_cores(jnp.where(odd, second, own))
        beside = over_views(own if near else across, 1)
        packs.append([own, first, second, across, beside])
    outs = grads = None
    for chunk in range(CHUNKS):
        outs, terms = attend(q, g, packs[chunk], outs, chunk)
        own, first, second, across, beside = terms
        handed = swap_cores(first)
        second = jnp.where(odd, add_two(second, handed), second)
        gathered = [handed, own, *two_back(second, RETURN_RELAYS[chunk])]
        back = over_views(beside, 1)
        if near:
            gathered += [back, over_views(across, far)]
        else:
            gathered.append(over_views(add_two(across, back), far))
        grads = add_up(gathered, grads, chunk, width)
    return tuple(x[None] for x in (*outs, *grads))


def add_two(a, b):
    return (a.astype(jnp.float32) + b.astype(jnp.float32)).astype(jnp.bfloat16)


def per_device(queries, keys, values, out_grad, counts, camera_pairs):
    first, second = camera_pairs[:, 0], camera_pairs[:, 1]
    met = jnp.sum(jnp.where(first == 0, second, 0)) + jnp.sum(jnp.where(second == 0, first, 0))
    apart = 6 - met
    plans = [(0, 2), (1, 3), (1, 2)]
    return lax.switch(
        apart - 1,
        [lambda *arrays, plan=plan: run(*plan, *arrays) for plan in plans],
        queries,
        keys,
        values,
        out_grad,
        counts,
    )


def solution(mesh):
    split = P("view", "clip", None)
    return jax.shard_map(
        per_device,
        mesh=mesh,
        in_specs=(split, split, split, split, P("view", "clip"), P()),
        out_specs=(split, split, split, split),
        check_vma=False,
    )
```

```python
import math

import jax
import jax.numpy as jnp
from jax import lax
from jax.experimental import pallas as pl
from jax.experimental.pallas import tpu as pltpu
from jax.sharding import PartitionSpec as P

H = 12
HD = 128
W = 2
NV = 4
GROUPS = ((4,), (8,))
PIECE = 4
PAD = 16
VMEM_BYTES = 16 * 1024 * 1024

MASKED = -1e30
FACTOR = 1.0 / math.sqrt(HD)
LOG2E = math.log2(math.e)


def dot(a, b, side_a, side_b):
    return lax.dot_general(
        a, b, (((side_a,), (side_b,)), ((), ())), preferred_element_type=jnp.float32
    )


def head_kernel(q_ref, g_ref, *refs):
    packs, (o_ref, dq_ref, *term_refs) = refs[: W + 3], refs[-(W + 5) :]
    rows = q_ref.shape[0]
    q = q_ref[...]
    g = g_ref[...]
    place = lax.broadcasted_iota(jnp.int32, (rows, rows), 0).astype(jnp.float32)
    scores, top = [], None
    for pack in packs:
        s = dot(pack[0:rows, :], q, 1, 1) * (FACTOR * LOG2E)
        count = pack[2 * rows : 2 * rows + 1, :].astype(jnp.float32)
        count = jnp.concatenate([count] * (rows // HD), axis=1)
        s = jnp.where(place < count, s, MASKED)
        scores.append(s)
        high = jnp.max(s, axis=0, keepdims=True)
        top = high if top is None else jnp.maximum(top, high)
    total, powers = 0.0, []
    for s in scores:
        power = jnp.exp2(s - top)
        powers.append(power)
        total = total + jnp.sum(power, axis=0, keepdims=True)
    inverse = 1.0 / total
    weights = [power * inverse for power in powers]
    low = [w.astype(jnp.bfloat16) for w in weights]
    out = 0.0
    for pack, w in zip(packs, low):
        out = out + dot(pack[rows : 2 * rows, :], w, 0, 0)
    out = out.astype(jnp.bfloat16)
    delta = jnp.sum(g.T.astype(jnp.float32) * out.astype(jnp.float32), axis=0, keepdims=True)
    o_ref[...] = out.T
    dq = 0.0
    for pack, w, w_low, term in zip(packs, weights, low, term_refs):
        dw = dot(pack[rows : 2 * rows, :], g, 1, 1)
        ds = (w * (dw - delta)).astype(jnp.bfloat16)
        dq = dq + dot(pack[0:rows, :], ds, 0, 0)
        term[0:rows, :] = (dot(ds, q, 1, 0) * FACTOR).astype(jnp.bfloat16)
        term[rows : 2 * rows, :] = dot(w_low, g, 1, 0).astype(jnp.bfloat16)
    dq_ref[...] = (dq * FACTOR).astype(jnp.bfloat16).T


def attend(q, g, packs, earlier, head, place, heads):
    rows, width = q.shape
    in_whole = pl.BlockSpec((rows, HD), lambda h: (0, head + h))
    in_pack = pl.BlockSpec((2 * rows + PAD, HD), lambda h: (0, place + h))
    term = pl.BlockSpec((2 * rows, HD), lambda h: (0, h))
    count = len(packs)
    arguments = [q, g, *packs]
    in_specs = [in_whole] * 2 + [in_pack] * count
    aliases = {}
    if earlier is not None:
        aliases = {len(arguments): 0, len(arguments) + 1: 1}
        arguments += list(earlier)
        in_specs += [pl.BlockSpec(memory_space=pl.ANY)] * 2
    results = pl.pallas_call(
        head_kernel,
        grid=(heads,),
        in_specs=in_specs,
        out_specs=[in_whole] * 2 + [term] * count,
        out_shape=[jax.ShapeDtypeStruct((rows, width), jnp.bfloat16)] * 2
        + [jax.ShapeDtypeStruct((2 * rows, heads * HD), jnp.bfloat16)] * count,
        input_output_aliases=aliases,
        cost_estimate=pl.CostEstimate(
            flops=0,
            bytes_accessed=0,
            transcendentals=0,
        ),
        compiler_params=pltpu.CompilerParams(vmem_limit_bytes=VMEM_BYTES),
    )(*arguments)
    return results[:2], results[2:]


def add_kernel(count, steps, even_ref, *refs):
    terms, pieces, (dk_ref, dv_ref) = refs[:count], refs[count : count + steps], refs[-2:]
    rows = dk_ref.shape[0]
    even = even_ref[0] == 1
    for at, piece in enumerate(pieces):

        @pl.when(pl.program_id(0) // PIECE == at)
        def _():
            for out, start in ((dk_ref, 0), (dv_ref, rows)):
                handed = terms[0][start : start + rows, :].astype(jnp.float32)
                total = jnp.where(even, handed, 0.0)
                for term in (*terms[1:], piece):
                    total = total + term[start : start + rows, :].astype(jnp.float32)
                out[...] = total.astype(jnp.bfloat16)


def add_up(terms, pieces, earlier, head, width):
    rows, part = terms[0].shape[0] // 2, terms[0].shape[1]
    count = len(terms)
    steps = part // HD
    in_specs = [pl.BlockSpec(memory_space=pltpu.SMEM)]
    in_specs += [pl.BlockSpec((2 * rows, HD), lambda h: (0, h))] * count
    for at in range(len(pieces)):
        place = lambda h, at=at: (0, jnp.clip(h - at * PIECE, 0, PIECE - 1))
        in_specs.append(pl.BlockSpec((2 * rows, HD), place))
    arguments = [even_clip(), *terms, *pieces]
    aliases = {}
    if earlier is not None:
        aliases = {len(arguments): 0, len(arguments) + 1: 1}
        arguments += list(earlier)
        in_specs += [pl.BlockSpec(memory_space=pl.ANY)] * 2
    return pl.pallas_call(
        lambda *refs: add_kernel(count, len(pieces), *refs),
        grid=(steps,),
        in_specs=in_specs,
        out_specs=[pl.BlockSpec((rows, HD), lambda h: (0, head + h))] * 2,
        out_shape=[jax.ShapeDtypeStruct((rows, width), jnp.bfloat16)] * 2,
        input_output_aliases=aliases,
        cost_estimate=pl.CostEstimate(flops=0, bytes_accessed=0, transcendentals=0),
        compiler_params=pltpu.CompilerParams(vmem_limit_bytes=VMEM_BYTES),
    )(*arguments)


def even_clip():
    return (1 - lax.axis_index("clip") % 2).astype(jnp.int32).reshape(1)


def over_views(block, flip):
    return lax.ppermute(block, "view", [(i, i ^ flip) for i in range(NV)])


def over_clips(block, route):
    return lax.ppermute(block, "clip", route)


def clip_at(z_hi, y, x, core):
    return ((z_hi * 4 + y) * 4 + x) * 2 + core


EDGE = 32
BEFORE, AFTER = (EDGE - 2, EDGE - 1), (EDGE, EDGE + 1)
OUTER = ((3, 3), (3, 2), (3, 0), (0, 3), (0, 0), (0, 1))
INNER = ((2, 3), (3, 1), (1, 0), (0, 2), (1, 3), (2, 0))


def by_relays(pieces, first, back):
    clips = lax.axis_size("clip")
    sources, targets = (AFTER, BEFORE) if back else (BEFORE, AFTER)
    hops = []
    for at, piece in enumerate(pieces, first):
        there, onward = [], []
        for view in range(NV):
            columns = OUTER if view in (0, NV - 1) else INNER
            for core in range(2):
                y, x = columns[2 * at + core]
                relay = clip_at(1, 3 - y, 3 - x, core) if back else clip_at(0, y, x, core)
                there.append((view * clips + sources[core], view * clips + relay))
                onward.append((view * clips + relay, view * clips + targets[core]))
        relayed = lax.ppermute(piece, ("view", "clip"), there)
        hops.append(lax.ppermute(relayed, ("view", "clip"), onward))
    return hops


def within_halves(block, distance):
    clips = range(lax.axis_size("clip"))
    route = [(i, i + distance) for i in clips if i + distance in clips]
    return over_clips(block, [(i, j) for i, j in route if i // EDGE == j // EDGE])


def swap_cores(block):
    return over_clips(block, [(i, i ^ 1) for i in range(lax.axis_size("clip"))])


def add_two(a, b):
    return (a.astype(jnp.float32) + b.astype(jnp.float32)).astype(jnp.bfloat16)


def pack(k, v, counts, head, heads):
    columns = slice(head * HD, (head + heads) * HD)
    count_rows = jnp.full((PAD, heads * HD), counts[0, 0], jnp.bfloat16)
    return jnp.concatenate([k[:, columns], v[:, columns], count_rows], axis=0)


def run(near, far, queries, keys, values, out_grad, counts):
    q, k, v, g = queries[0], keys[0], values[0], out_grad[0]
    rows, width = q.shape
    clip = lax.axis_index("clip")
    odd = clip % 2 == 1
    after_edge = (clip == EDGE) | (clip == EDGE + 1)

    def fetch(head, heads):
        own = pack(k, v, counts, head, heads)
        pieces = [pack(k, v, counts, at, PIECE) for at in range(head, head + heads, PIECE)]
        crossed = by_relays(pieces, head // PIECE, False)
        within = within_halves(own, 2)
        across = over_views(own, far)
        beside = over_views(own if near else across, 1)
        crossed = crossed[0] if len(crossed) == 1 else jnp.concatenate(crossed, axis=1)
        return own, (within, crossed, across, beside)

    def gather(own, arrived):
        within, crossed, across, beside = arrived
        second = jnp.where(after_edge, crossed, within)
        first = swap_cores(jnp.where(odd, second, own))
        return [own, first, second, across, beside]

    def hand_back(terms, head, heads, others):
        own, first, second, across, beside = terms
        first, *others = lax.optimization_barrier((first, *others))
        handed = swap_cores(first)
        second = jnp.where(odd, add_two(second, handed), second)
        pieces = [second[:, i * HD : (i + PIECE) * HD] for i in range(0, heads, PIECE)]
        crossed = by_relays(pieces, head // PIECE, True)
        back = over_views(beside, 1)
        by_clip = [handed, own, within_halves(second, -2)]
        if near:
            return by_clip, crossed, [back, over_views(across, far)], others
        return by_clip, crossed, [over_views(add_two(across, back), far)], others

    heads_of = [sum(parts) for parts in GROUPS]
    starts = [sum(heads_of[:i]) for i in range(len(GROUPS))]
    fetched = [fetch(*x) for x in zip(starts, heads_of)]
    outs = None
    done, by_view, waiting = [], [], None
    for group, parts in enumerate(GROUPS):
        own, arrived = fetched[group]
        if waiting is None:
            arrived = lax.optimization_barrier(arrived)
        else:
            terms, *at = waiting
            arrived, terms = lax.optimization_barrier((arrived, terms))
            *sent, by_view, _ = hand_back(terms, *at, by_view)
            done.append([*at, *sent, by_view])
        packs = gather(own, arrived)
        place = 0
        for part, heads in enumerate(parts):
            head = starts[group] + place
            outs, terms = attend(q, g, packs, outs, head, place, heads)
            place += heads
            waiting = (terms, head, heads)
            if part + 1 < len(parts) or group + 1 == len(GROUPS):
                *sent, by_view, early = hand_back(*waiting, by_view)
                if done:
                    done[-1][-1] = early
                done.append([head, heads, *sent, by_view])
    grads = None
    for head, heads, by_clip, crossed, by_view in done:
        grads = add_up(by_clip + by_view, crossed, grads, head, width)
    return lax.optimization_barrier(tuple(x[None] for x in (*outs, *grads)))


def per_device(queries, keys, values, out_grad, counts, camera_pairs):
    first, second = camera_pairs[:, 0], camera_pairs[:, 1]
    met = jnp.sum(jnp.where(first == 0, second, 0)) + jnp.sum(jnp.where(second == 0, first, 0))
    apart = 6 - met
    plans = [(0, 2), (1, 3), (1, 2)]
    return lax.switch(
        apart - 1,
        [lambda *arrays, plan=plan: run(*plan, *arrays) for plan in plans],
        queries,
        keys,
        values,
        out_grad,
        counts,
    )


def solution(mesh):
    split = P("view", "clip", None)
    return jax.shard_map(
        per_device,
        mesh=mesh,
        in_specs=(split, split, split, split, P("view", "clip"), P()),
        out_specs=(split, split, split, split),
        check_vma=False,
    )
```

```python
import math

import jax
import jax.numpy as jnp
from jax import lax
from jax.experimental import pallas as pl
from jax.experimental.pallas import tpu as pltpu
from jax.sharding import PartitionSpec as P

H = 12
HD = 128
W = 2
NV = 4
GROUPS = (4, 8)
PIECE = 4
HEADS_AT_ONCE = 2
PAD = 16
VMEM_BYTES = 24 * 1024 * 1024

MASKED = -1e30
FACTOR = 1.0 / math.sqrt(HD)
LOG2E = math.log2(math.e)


def dot(a, b, side_a, side_b):
    return lax.dot_general(
        a, b, (((side_a,), (side_b,)), ((), ())), preferred_element_type=jnp.float32
    )


def softmax_parts(q, packs, columns):
    rows = q.shape[0]
    place = lax.broadcasted_iota(jnp.int32, (rows, rows), 0).astype(jnp.float32)
    scores, top = [], None
    for pack in packs:
        s = dot(pack[0:rows, columns], q, 1, 1) * (FACTOR * LOG2E)
        count = pack[2 * rows : 2 * rows + 1, columns].astype(jnp.float32)
        count = jnp.concatenate([count] * (rows // HD), axis=1)
        s = jnp.where(place < count, s, MASKED)
        scores.append(s)
        high = jnp.max(s, axis=0, keepdims=True)
        top = high if top is None else jnp.maximum(top, high)
    return scores, top


def weights_of(scores, top):
    total, powers = 0.0, []
    for s in scores:
        power = jnp.exp2(s - top)
        powers.append(power)
        total = total + jnp.sum(power, axis=0, keepdims=True)
    inverse = 1.0 / total
    weights = [power * inverse for power in powers]
    return weights, [w.astype(jnp.bfloat16) for w in weights]


def head_kernel(q_ref, g_ref, *refs):
    packs, (o_ref, dq_ref, *term_refs) = refs[: W + 3], refs[-(W + 5) :]
    rows = q_ref.shape[0]
    heads = [slice(i * HD, (i + 1) * HD) for i in range(HEADS_AT_ONCE)]
    parts = [softmax_parts(q_ref[:, columns], packs, columns) for columns in heads]
    soft = [weights_of(*part) for part in parts]
    for columns, (weights, low) in zip(heads, soft):
        q = q_ref[:, columns]
        g = g_ref[:, columns]
        out = 0.0
        for pack, w in zip(packs, low):
            out = out + dot(pack[rows : 2 * rows, columns], w, 0, 0)
        out = out.astype(jnp.bfloat16)
        delta = jnp.sum(g.T.astype(jnp.float32) * out.astype(jnp.float32), axis=0, keepdims=True)
        o_ref[:, columns] = out.T
        dq = 0.0
        for pack, w, w_low, term in zip(packs, weights, low, term_refs):
            dw = dot(pack[rows : 2 * rows, columns], g, 1, 1)
            ds = (w * (dw - delta)).astype(jnp.bfloat16)
            dq = dq + dot(pack[0:rows, columns], ds, 0, 0)
            term[0:rows, columns] = (dot(ds, q, 1, 0) * FACTOR).astype(jnp.bfloat16)
            term[rows : 2 * rows, columns] = dot(w_low, g, 1, 0).astype(jnp.bfloat16)
        dq_ref[:, columns] = (dq * FACTOR).astype(jnp.bfloat16).T


def attend(q, g, packs, earlier, head, heads):
    rows, width = q.shape
    lanes = HEADS_AT_ONCE * HD
    in_whole = pl.BlockSpec((rows, lanes), lambda h: (0, head // HEADS_AT_ONCE + h))
    in_pack = pl.BlockSpec((2 * rows + PAD, lanes), lambda h: (0, h))
    term = pl.BlockSpec((2 * rows, lanes), lambda h: (0, h))
    count = len(packs)
    arguments = [q, g, *packs]
    in_specs = [in_whole] * 2 + [in_pack] * count
    aliases = {}
    if earlier is not None:
        aliases = {len(arguments): 0, len(arguments) + 1: 1}
        arguments += list(earlier)
        in_specs += [pl.BlockSpec(memory_space=pl.ANY)] * 2
    results = pl.pallas_call(
        head_kernel,
        grid=(heads // HEADS_AT_ONCE,),
        in_specs=in_specs,
        out_specs=[in_whole] * 2 + [term] * count,
        out_shape=[jax.ShapeDtypeStruct((rows, width), jnp.bfloat16)] * 2
        + [jax.ShapeDtypeStruct((2 * rows, heads * HD), jnp.bfloat16)] * count,
        input_output_aliases=aliases,
        cost_estimate=pl.CostEstimate(
            flops=0,
            bytes_accessed=0,
            transcendentals=0,
        ),
        compiler_params=pltpu.CompilerParams(vmem_limit_bytes=VMEM_BYTES),
    )(*arguments)
    return results[:2], list(results[2:])


def add_kernel(count, steps, even_ref, *refs):
    terms, pieces, (dk_ref, dv_ref) = refs[:count], refs[count : len(refs) - 2], refs[-2:]
    rows = dk_ref.shape[0]
    even = even_ref[0] == 1
    for at in range(steps):

        @pl.when(pl.program_id(0) // (PIECE // HEADS_AT_ONCE) == at)
        def _():
            for out, start in ((dk_ref, 0), (dv_ref, rows)):
                handed = terms[0][start : start + rows, :].astype(jnp.float32)
                total = jnp.where(even, handed, 0.0)
                for term in (*terms[1:], *pieces[at::steps]):
                    total = total + term[start : start + rows, :].astype(jnp.float32)
                out[...] = total.astype(jnp.bfloat16)


def add_up(terms, pieces, earlier, head, width):
    rows, part = terms[0].shape[0] // 2, terms[0].shape[1]
    count, steps = len(terms), part // (PIECE * HD)
    lanes, in_piece = HEADS_AT_ONCE * HD, PIECE // HEADS_AT_ONCE
    in_specs = [pl.BlockSpec(memory_space=pltpu.SMEM)]
    in_specs += [pl.BlockSpec((2 * rows, lanes), lambda h: (0, h))] * count
    for at in range(len(pieces)):
        place = lambda h, at=at % steps: (0, jnp.clip(h - at * in_piece, 0, in_piece - 1))
        in_specs.append(pl.BlockSpec((2 * rows, lanes), place))
    arguments = [even_clip(), *terms, *pieces]
    aliases = {}
    if earlier is not None:
        aliases = {len(arguments): 0, len(arguments) + 1: 1}
        arguments += list(earlier)
        in_specs += [pl.BlockSpec(memory_space=pl.ANY)] * 2

    def kernel(*refs):
        inputs = refs[: 1 + count + len(pieces)]
        add_kernel(count, steps, *inputs, *refs[-2:])

    return pl.pallas_call(
        kernel,
        grid=(part // lanes,),
        in_specs=in_specs,
        out_specs=[pl.BlockSpec((rows, lanes), lambda h: (0, head // HEADS_AT_ONCE + h))] * 2,
        out_shape=[jax.ShapeDtypeStruct((rows, width), jnp.bfloat16)] * 2,
        input_output_aliases=aliases,
        cost_estimate=pl.CostEstimate(flops=0, bytes_accessed=0, transcendentals=0),
        compiler_params=pltpu.CompilerParams(vmem_limit_bytes=VMEM_BYTES),
    )(*arguments)


def even_clip():
    return (1 - lax.axis_index("clip") % 2).astype(jnp.int32).reshape(1)


def over_views(block, flip):
    return lax.ppermute(block, "view", [(i, i ^ flip) for i in range(NV)])


def over_clips(block, route):
    return lax.ppermute(block, "clip", route)


def clip_at(z_hi, y, x, core):
    return ((z_hi * 4 + y) * 4 + x) * 2 + core


EDGE = 32
BEFORE, AFTER = (EDGE - 2, EDGE - 1), (EDGE, EDGE + 1)
OUTER = ((3, 3), (3, 2), (3, 0), (0, 3), (0, 0), (0, 1))
INNER = ((2, 3), (3, 1), (1, 0), (0, 2), (1, 3), (2, 0))


def by_relays(pieces, first, back):
    clips = lax.axis_size("clip")
    sources, targets = (AFTER, BEFORE) if back else (BEFORE, AFTER)
    hops = []
    for at, piece in enumerate(pieces, first):
        there, onward = [], []
        for view in range(NV):
            columns = OUTER if view in (0, NV - 1) else INNER
            for core in range(2):
                y, x = columns[2 * at + core]
                relay = clip_at(1, 3 - y, 3 - x, core) if back else clip_at(0, y, x, core)
                there.append((view * clips + sources[core], view * clips + relay))
                onward.append((view * clips + relay, view * clips + targets[core]))
        relayed = lax.ppermute(piece, ("view", "clip"), there)
        hops.append(lax.ppermute(relayed, ("view", "clip"), onward))
    return hops


def within_halves(block, distance):
    clips = range(lax.axis_size("clip"))
    route = [(i, i + distance) for i in clips if i + distance in clips]
    return over_clips(block, [(i, j) for i, j in route if i // EDGE == j // EDGE])


def swap_cores(block):
    return over_clips(block, [(i, i ^ 1) for i in range(lax.axis_size("clip"))])


def add_two(a, b):
    return (a.astype(jnp.float32) + b.astype(jnp.float32)).astype(jnp.bfloat16)


def pack(k, v, counts, head, heads):
    columns = slice(head * HD, (head + heads) * HD)
    count_rows = jnp.full((PAD, heads * HD), counts[0, 0], jnp.bfloat16)
    return jnp.concatenate([k[:, columns], v[:, columns], count_rows], axis=0)


def run(near, far, queries, keys, values, out_grad, counts):
    q, k, v, g = queries[0], keys[0], values[0], out_grad[0]
    rows, width = q.shape
    clip = lax.axis_index("clip")
    odd = clip % 2 == 1
    after_edge = (clip == EDGE) | (clip == EDGE + 1)

    def fetch(head, heads):
        own = pack(k, v, counts, head, heads)
        pieces = [pack(k, v, counts, at, PIECE) for at in range(head, head + heads, PIECE)]
        crossed = by_relays(pieces, head // PIECE, False)
        within = within_halves(own, 2)
        across = over_views(own, far)
        beside = over_views(own if near else across, 1)
        crossed = crossed[0] if len(crossed) == 1 else jnp.concatenate(crossed, axis=1)
        return own, (within, crossed, across, beside)

    def gather(own, arrived, after_this):
        within, crossed, across, beside = arrived
        second = jnp.where(after_edge, crossed, within)
        if not near:
            second, *after_this = lax.optimization_barrier((second, *after_this))
        first = swap_cores(jnp.where(odd, second, own))
        return [own, first, second, across, beside], after_this

    def split(block):
        return [block[:, i * HD : (i + PIECE) * HD] for i in range(0, block.shape[1] // HD, PIECE)]

    def back_by_clips(terms, head):
        first, second = terms[1:3]
        handed = swap_cores(first)
        second = jnp.where(odd, add_two(second, handed), second)
        return handed, within_halves(second, -2), by_relays(split(second), head // PIECE, True)

    def back_by_views(terms):
        across, beside = terms[3:]
        if near:
            return [over_views(beside, 1), over_views(across, far)], []
        pieces = []
        for a, b in zip(split(across), split(beside)):
            pieces.append(over_views(add_two(a, over_views(b, 1)), far))
        return [], pieces

    small, large = GROUPS
    own, arrived = fetch(0, small)
    own_last, arrived_last = fetch(small, large)
    packs, _ = gather(own, lax.optimization_barrier(arrived), [])
    outs, terms = attend(q, g, packs, None, 0, small)
    arrived_last, outs = lax.optimization_barrier((arrived_last, outs))
    handed, within, crossed = back_by_clips(terms, 0)
    whole, pieces = back_by_views(terms)
    packs, within_late = gather(own_last, arrived_last, [within])
    within = within if near else within_late[0]
    outs, terms_last = attend(q, g, packs, outs, small, large)
    terms_last[1], whole, pieces = lax.optimization_barrier((terms_last[1], whole, pieces))
    handed_last, within_last, crossed_last = back_by_clips(terms_last, small)
    whole_last, pieces_last = back_by_views(terms_last)
    grads = add_up([handed, terms[0], within, *whole], crossed + pieces, None, 0, width)
    last = [handed_last, terms_last[0], within_last, *whole_last]
    grads = add_up(last, crossed_last + pieces_last, grads, small, width)
    return lax.optimization_barrier(tuple(x[None] for x in (*outs, *grads)))


def per_device(queries, keys, values, out_grad, counts, camera_pairs):
    first, second = camera_pairs[:, 0], camera_pairs[:, 1]
    met = jnp.sum(jnp.where(first == 0, second, 0)) + jnp.sum(jnp.where(second == 0, first, 0))
    apart = 6 - met
    plans = [(0, 2), (1, 3), (1, 2)]
    return lax.switch(
        apart - 1,
        [lambda *arrays, plan=plan: run(*plan, *arrays) for plan in plans],
        queries,
        keys,
        values,
        out_grad,
        counts,
    )


def solution(mesh):
    split = P("view", "clip", None)
    return jax.shard_map(
        per_device,
        mesh=mesh,
        in_specs=(split, split, split, split, P("view", "clip"), P()),
        out_specs=(split, split, split, split),
        check_vma=False,
    )
```

```python
import math

import jax
import jax.numpy as jnp
from jax import lax
from jax.experimental import pallas as pl
from jax.experimental.pallas import tpu as pltpu
from jax.sharding import PartitionSpec as P

H = 12
HD = 128
W = 2
NV = 4
GROUPS = (4, 8)
PIECE = 4
HEADS_AT_ONCE = 2
PAD = 16
VMEM_BYTES = 24 * 1024 * 1024

MASKED = -1e30
FACTOR = 1.0 / math.sqrt(HD)
LOG2E = math.log2(math.e)


def dot(a, b, side_a, side_b):
    return lax.dot_general(
        a, b, (((side_a,), (side_b,)), ((), ())), preferred_element_type=jnp.float32
    )


def softmax_parts(q, packs, columns):
    rows = q.shape[0]
    place = lax.broadcasted_iota(jnp.int32, (rows, rows), 0).astype(jnp.float32)
    scores, top = [], None
    for pack in packs:
        s = dot(pack[0:rows, columns], q, 1, 1) * (FACTOR * LOG2E)
        count = pack[2 * rows : 2 * rows + 1, columns].astype(jnp.float32)
        count = jnp.concatenate([count] * (rows // HD), axis=1)
        s = jnp.where(place < count, s, MASKED)
        scores.append(s)
        high = jnp.max(s, axis=0, keepdims=True)
        top = high if top is None else jnp.maximum(top, high)
    return scores, top


def weights_of(scores, top):
    total, powers = 0.0, []
    for s in scores:
        power = jnp.exp2(s - top)
        powers.append(power)
        total = total + jnp.sum(power, axis=0, keepdims=True)
    inverse = 1.0 / total
    weights = [power * inverse for power in powers]
    return weights, [w.astype(jnp.bfloat16) for w in weights]


def head_kernel(q_ref, g_ref, *refs):
    packs, (o_ref, dq_ref, *term_refs) = refs[: W + 3], refs[-(W + 5) :]
    rows = q_ref.shape[0]
    heads = [slice(i * HD, (i + 1) * HD) for i in range(HEADS_AT_ONCE)]
    parts = [softmax_parts(q_ref[:, columns], packs, columns) for columns in heads]
    soft = [weights_of(*part) for part in parts]
    for columns, (weights, low) in zip(heads, soft):
        q = q_ref[:, columns]
        g = g_ref[:, columns]
        out = 0.0
        for pack, w in zip(packs, low):
            out = out + dot(pack[rows : 2 * rows, columns], w, 0, 0)
        out = out.astype(jnp.bfloat16)
        delta = jnp.sum(g.T.astype(jnp.float32) * out.astype(jnp.float32), axis=0, keepdims=True)
        o_ref[:, columns] = out.T
        dq = 0.0
        for pack, w, w_low, term in zip(packs, weights, low, term_refs):
            dw = dot(pack[rows : 2 * rows, columns], g, 1, 1)
            ds = (w * (dw - delta)).astype(jnp.bfloat16)
            dq = dq + dot(pack[0:rows, columns], ds, 0, 0)
            term[0:rows, columns] = (dot(ds, q, 1, 0) * FACTOR).astype(jnp.bfloat16)
            term[rows : 2 * rows, columns] = dot(w_low, g, 1, 0).astype(jnp.bfloat16)
        dq_ref[:, columns] = (dq * FACTOR).astype(jnp.bfloat16).T


def attend(q, g, packs, earlier, head, heads):
    rows, width = q.shape
    lanes = HEADS_AT_ONCE * HD
    in_whole = pl.BlockSpec((rows, lanes), lambda h: (0, head // HEADS_AT_ONCE + h))
    in_pack = pl.BlockSpec((2 * rows + PAD, lanes), lambda h: (0, h))
    term = pl.BlockSpec((2 * rows, lanes), lambda h: (0, h))
    count = len(packs)
    arguments = [q, g, *packs]
    in_specs = [in_whole] * 2 + [in_pack] * count
    aliases = {}
    if earlier is not None:
        aliases = {len(arguments): 0, len(arguments) + 1: 1}
        arguments += list(earlier)
        in_specs += [pl.BlockSpec(memory_space=pl.ANY)] * 2
    results = pl.pallas_call(
        head_kernel,
        grid=(heads // HEADS_AT_ONCE,),
        in_specs=in_specs,
        out_specs=[in_whole] * 2 + [term] * count,
        out_shape=[jax.ShapeDtypeStruct((rows, width), jnp.bfloat16)] * 2
        + [jax.ShapeDtypeStruct((2 * rows, heads * HD), jnp.bfloat16)] * count,
        input_output_aliases=aliases,
        cost_estimate=pl.CostEstimate(
            flops=0,
            bytes_accessed=0,
            transcendentals=0,
        ),
        compiler_params=pltpu.CompilerParams(vmem_limit_bytes=VMEM_BYTES),
    )(*arguments)
    return results[:2], list(results[2:])


def add_kernel(count, steps, even_ref, *refs):
    terms, pieces, (dk_ref, dv_ref) = refs[:count], refs[count : len(refs) - 2], refs[-2:]
    rows = dk_ref.shape[0]
    even = even_ref[0] == 1
    for at in range(steps):

        @pl.when(pl.program_id(0) // (PIECE // HEADS_AT_ONCE) == at)
        def _():
            for out, start in ((dk_ref, 0), (dv_ref, rows)):
                handed = terms[0][start : start + rows, :].astype(jnp.float32)
                total = jnp.where(even, handed, 0.0)
                for term in (*terms[1:], *pieces[at::steps]):
                    total = total + term[start : start + rows, :].astype(jnp.float32)
                out[...] = total.astype(jnp.bfloat16)


def add_up(terms, pieces, earlier, head, width):
    rows, part = terms[0].shape[0] // 2, terms[0].shape[1]
    count, steps = len(terms), part // (PIECE * HD)
    lanes, in_piece = HEADS_AT_ONCE * HD, PIECE // HEADS_AT_ONCE
    in_specs = [pl.BlockSpec(memory_space=pltpu.SMEM)]
    in_specs += [pl.BlockSpec((2 * rows, lanes), lambda h: (0, h))] * count
    for at in range(len(pieces)):
        place = lambda h, at=at % steps: (0, jnp.clip(h - at * in_piece, 0, in_piece - 1))
        in_specs.append(pl.BlockSpec((2 * rows, lanes), place))
    arguments = [even_clip(), *terms, *pieces]
    aliases = {}
    if earlier is not None:
        aliases = {len(arguments): 0, len(arguments) + 1: 1}
        arguments += list(earlier)
        in_specs += [pl.BlockSpec(memory_space=pl.ANY)] * 2

    def kernel(*refs):
        inputs = refs[: 1 + count + len(pieces)]
        add_kernel(count, steps, *inputs, *refs[-2:])

    return pl.pallas_call(
        kernel,
        grid=(part // lanes,),
        in_specs=in_specs,
        out_specs=[pl.BlockSpec((rows, lanes), lambda h: (0, head // HEADS_AT_ONCE + h))] * 2,
        out_shape=[jax.ShapeDtypeStruct((rows, width), jnp.bfloat16)] * 2,
        input_output_aliases=aliases,
        cost_estimate=pl.CostEstimate(flops=0, bytes_accessed=0, transcendentals=0),
        compiler_params=pltpu.CompilerParams(vmem_limit_bytes=VMEM_BYTES),
    )(*arguments)


def even_clip():
    return (1 - lax.axis_index("clip") % 2).astype(jnp.int32).reshape(1)


def over_views(block, flip):
    return lax.ppermute(block, "view", [(i, i ^ flip) for i in range(NV)])


def over_clips(block, route):
    return lax.ppermute(block, "clip", route)


def clip_at(z_hi, y, x, core):
    return ((z_hi * 4 + y) * 4 + x) * 2 + core


EDGE = 32
BEFORE, AFTER = (EDGE - 2, EDGE - 1), (EDGE, EDGE + 1)
OUTER = ((3, 3), (3, 2), (3, 0), (0, 3), (0, 0), (0, 1))
INNER = ((2, 3), (3, 1), (1, 0), (0, 2), (1, 3), (2, 0))


def by_relays(pieces, first, back):
    clips = lax.axis_size("clip")
    sources, targets = (AFTER, BEFORE) if back else (BEFORE, AFTER)
    hops = []
    for at, piece in enumerate(pieces, first):
        there, onward = [], []
        for view in range(NV):
            columns = OUTER if view in (0, NV - 1) else INNER
            for core in range(2):
                y, x = columns[2 * at + core]
                relay = clip_at(1, 3 - y, 3 - x, core) if back else clip_at(0, y, x, core)
                there.append((view * clips + sources[core], view * clips + relay))
                onward.append((view * clips + relay, view * clips + targets[core]))
        relayed = lax.ppermute(piece, ("view", "clip"), there)
        hops.append(lax.ppermute(relayed, ("view", "clip"), onward))
    return hops


def within_halves(block, distance):
    clips = range(lax.axis_size("clip"))
    route = [(i, i + distance) for i in clips if i + distance in clips]
    return over_clips(block, [(i, j) for i, j in route if i // EDGE == j // EDGE])


def swap_cores(block):
    return over_clips(block, [(i, i ^ 1) for i in range(lax.axis_size("clip"))])


def add_two(a, b):
    return (a.astype(jnp.float32) + b.astype(jnp.float32)).astype(jnp.bfloat16)


def pack(k, v, counts, head, heads):
    columns = slice(head * HD, (head + heads) * HD)
    count_rows = jnp.full((PAD, heads * HD), counts[0, 0], jnp.bfloat16)
    return jnp.concatenate([k[:, columns], v[:, columns], count_rows], axis=0)


def run(near, far, queries, keys, values, out_grad, counts):
    q, k, v, g = queries[0], keys[0], values[0], out_grad[0]
    rows, width = q.shape
    clip = lax.axis_index("clip")
    odd = clip % 2 == 1
    after_edge = (clip == EDGE) | (clip == EDGE + 1)

    def fetch(head, heads):
        own = pack(k, v, counts, head, heads)
        pieces = [pack(k, v, counts, at, PIECE) for at in range(head, head + heads, PIECE)]
        crossed = by_relays(pieces, head // PIECE, False)
        within = within_halves(own, 2)
        across = over_views(own, far)
        beside = over_views(own if near else across, 1)
        crossed = crossed[0] if len(crossed) == 1 else jnp.concatenate(crossed, axis=1)
        return own, (within, crossed, across, beside)

    def gather(own, arrived, after_this):
        within, crossed, across, beside = arrived
        second = jnp.where(after_edge, crossed, within)
        if not near:
            second, *after_this = lax.optimization_barrier((second, *after_this))
        first = swap_cores(jnp.where(odd, second, own))
        return [own, first, second, across, beside], after_this

    def split(block):
        return [block[:, i * HD : (i + PIECE) * HD] for i in range(0, block.shape[1] // HD, PIECE)]

    def back_by_clips(terms, head):
        first, second = terms[1:3]
        handed = swap_cores(first)
        second = jnp.where(odd, add_two(second, handed), second)
        return handed, within_halves(second, -2), by_relays(split(second), head // PIECE, True)

    def back_by_views(terms):
        across, beside = terms[3:]
        if near:
            far_terms = over_views(across, far)
            return [far_terms, over_views(beside, 1)], []
        backs = []
        for piece in split(beside):
            if backs:
                piece, backs[-1] = lax.optimization_barrier((piece, backs[-1]))
            backs.append(over_views(piece, 1))
        pieces = zip(split(across), backs)
        return [], [over_views(add_two(a, b), far) for a, b in pieces]

    small, large = GROUPS
    own, arrived = fetch(0, small)
    own_last, arrived_last = fetch(small, large)
    packs, _ = gather(own, lax.optimization_barrier(arrived), [])
    outs, terms = attend(q, g, packs, None, 0, small)
    arrived_last, outs = lax.optimization_barrier((arrived_last, outs))
    handed, within, crossed = back_by_clips(terms, 0)
    whole, pieces = back_by_views(terms)
    packs, within_late = gather(own_last, arrived_last, [within])
    within = within if near else within_late[0]
    outs, terms_last = attend(q, g, packs, outs, small, large)
    terms_last[1], whole, pieces = lax.optimization_barrier((terms_last[1], whole, pieces))
    handed_last, within_last, crossed_last = back_by_clips(terms_last, small)
    whole_last, pieces_last = back_by_views(terms_last)
    grads = add_up([handed, terms[0], within, *whole], crossed + pieces, None, 0, width)
    last = [handed_last, terms_last[0], within_last, *whole_last]
    grads = add_up(last, crossed_last + pieces_last, grads, small, width)
    return lax.optimization_barrier(tuple(x[None] for x in (*outs, *grads)))


def per_device(queries, keys, values, out_grad, counts, camera_pairs):
    first, second = camera_pairs[:, 0], camera_pairs[:, 1]
    met = jnp.sum(jnp.where(first == 0, second, 0)) + jnp.sum(jnp.where(second == 0, first, 0))
    apart = 6 - met
    plans = [(0, 2), (1, 3), (1, 2)]
    return lax.switch(
        apart - 1,
        [lambda *arrays, plan=plan: run(*plan, *arrays) for plan in plans],
        queries,
        keys,
        values,
        out_grad,
        counts,
    )


def solution(mesh):
    split = P("view", "clip", None)
    return jax.shard_map(
        per_device,
        mesh=mesh,
        in_specs=(split, split, split, split, P("view", "clip"), P()),
        out_specs=(split, split, split, split),
        check_vma=False,
    )
```
